32 devices in a mesh: space: 4 (over y, core), ctx: 8 (over z, x).
Axes of the slice: x: 2, y: 2, z: 4, core: 2. Of those that a mesh axis runs over, the one named last changes fastest.
Arguments:
- feats: bfloat16 [4, 8192, 256], P('space', 'ctx'), may hold values from -6 to 6
- face_rows: int32 [4, 2048], P('space', 'ctx'), may hold values from 0 to 1023
- neighbours: int32 [4, 8192, 6], P('space', 'ctx'), may hold values from 0 to 2048
- block_len: int32 [4, 64], P('space'), may hold values from 32 to 128
- dilated: int32 [4, 64, 4], P('space', 'ctx'), may hold values from 0 to 7, as said below
- pick: int32 [4, 8, 8], P('space'), may hold values from 0 to 7
- cpe_weight: bfloat16 [7, 256, 256], replicated, may hold values from -0.125 to 0.125
- cpe_bias: float32 [256], replicated, may hold values from -3 to 3
- ln_gain: float32 [256], replicated, may hold values from 0.1 to 1.9
- ln_bias: float32 [256], replicated, may hold values from -3 to 3
- w_qkv: bfloat16 [256, 768], replicated, may hold values from -11 to 11
- w_out: bfloat16 [256, 256], replicated, may hold values from -3 to 3
Outputs:
- mixed: bfloat16 [4, 8192, 256], P('space', 'ctx')
The draws below stay inside these ranges and needn't reach their ends.
Inputs may be any that keep to these rules, and one draw needn't show every extreme that they name: `dilated`: among the 32 entries of the blocks of one range, every value 0 to 7 appears.
All inputs are finite; a program needn't handle non-finite values.
Results may differ from the reference program's by a relative error of at most 0.009.
The reference program's roundings to bfloat16 on the way count: a program that leaves them out, or rounds other values in their place, can miss the bound.
Values may be sent and summed in bfloat16 or wider, within the bound.
A program may use at most 128 MiB of HBM per device.

```python
import math
import jax
import jax.numpy as jnp
from jax import lax

D = 256
HEADS = 8
BLK = 128
DILATED_BLOCKS = 4
EDGE = 128
FACE = 256
VOX_DEV = 1024
SCENE_TILES = 4
SEQ = 8192
RANGE_BLOCKS = 8
TILE_BLOCKS = 64
N_SPACE = 4
N_CTX = 8


def draw_neighbours(key, part):
    keys_all = jax.random.split(key, 6)
    draw_shape = (SCENE_TILES, SEQ, 6)
    block_category = jax.random.randint(keys_all[0], draw_shape, 0, 20)
    lower_edge = jax.random.randint(keys_all[1], draw_shape, 0, EDGE)
    upper_edge = jax.random.randint(keys_all[2], draw_shape, EDGE + VOX_DEV, 2 * EDGE + VOX_DEV)
    face_start = VOX_DEV + 2 * EDGE
    lower_face = jax.random.randint(keys_all[3], draw_shape, face_start, face_start + FACE)
    upper_face = jax.random.randint(keys_all[4], draw_shape, face_start + 2 * FACE, face_start + 3 * FACE)
    own_rows = jax.random.randint(keys_all[5], draw_shape, EDGE, EDGE + VOX_DEV)
    missing = face_start + 3 * FACE
    selected_keys = jnp.where(block_category < 11, upper_face, own_rows)
    selected_keys = jnp.where(block_category < 9, lower_face, selected_keys)
    selected_keys = jnp.where(block_category < 7, upper_edge, selected_keys)
    selected_keys = jnp.where(block_category < 5, lower_edge, selected_keys)
    selected_keys = jnp.where(block_category < 3, missing, selected_keys)
    return selected_keys.astype(jnp.int32)


def draw_block_len(key, part):
    keys_all = jax.random.split(key, 3)
    lengths = jax.random.randint(keys_all[0], (SCENE_TILES, TILE_BLOCKS), BLK // 4, BLK + 1)
    first_col = jax.random.randint(keys_all[1], (SCENE_TILES,), 0, TILE_BLOCKS)
    second_col = (first_col + 1 + jax.random.randint(keys_all[2], (SCENE_TILES,), 0, TILE_BLOCKS - 1)) % TILE_BLOCKS
    tile_ids = jnp.arange(SCENE_TILES)
    lengths = lengths.at[tile_ids, first_col].set(BLK)
    lengths = lengths.at[tile_ids, second_col].set(BLK // 4)
    return lengths.astype(jnp.int32)


def draw_dilated(key, part):
    subkeys = jax.random.split(key, SCENE_TILES * N_CTX)
    orders = jax.vmap(lambda subkey: jax.random.permutation(subkey, N_CTX))(subkeys).astype(jnp.int32)
    memory_reads = jnp.arange(RANGE_BLOCKS * DILATED_BLOCKS) % N_CTX
    selected_keys = orders[:, memory_reads]
    return selected_keys.reshape(SCENE_TILES, TILE_BLOCKS, DILATED_BLOCKS).astype(jnp.int32)


def draw_w_qkv(key, part):
    keys_all = jax.random.split(key, 3)
    norm_scale = D ** (-0.5)
    w_key = jnp.clip(jax.random.normal(keys_all[0], (D, D), jnp.float32), -4.0, 4.0) * norm_scale
    w_value = jnp.clip(jax.random.normal(keys_all[1], (D, D), jnp.float32), -4.0, 4.0) * norm_scale
    noise = jnp.clip(jax.random.normal(keys_all[2], (D, D), jnp.float32), -4.0, 4.0) * norm_scale
    w_query = noise
    return jnp.concatenate([w_query, w_key, w_value], 1).astype(jnp.bfloat16)


def with_ends(result, stream_key, low, high):
    longest = result.shape.index(max(result.shape))
    spots = []
    for shift in (0, 1):
        where = [jax.random.randint(jax.random.fold_in(stream_key, axis), (), 0, length) for axis, length in enumerate(result.shape)]
        where[longest] = (where[longest] + shift) % result.shape[longest]
        spots.append(tuple(where))
    return result.at[spots[0]].set(low).at[spots[1]].set(high)


def block_levels(own_key, extent, pieces, low, high):
    level, own = 1.0, jax.random.fold_in(own_key, 6)
    for axis_at, parts in pieces:
        draws = jnp.exp(jax.random.uniform(jax.random.fold_in(own, axis_at), (parts,), jnp.float32, low / len(pieces), high / len(pieces)))
        level = level * jnp.repeat(draws, extent[axis_at] // parts).reshape([-1 if axis == axis_at else 1 for axis in range(len(extent))])
    return level


def normal_values(key, extent, width, limit, shards=(), kind=jnp.bfloat16):
    factor_of = block_levels(key, extent, shards, -0.22, 0.18) if shards else 1.0
    entries = jax.random.normal(key, extent, jnp.float32) * width * factor_of
    return jnp.minimum(jnp.maximum(entries, -limit), limit).astype(kind)


def setup_inputs(seed: int = 0) -> dict:
    splits = jax.random.split(jax.random.key(seed), 13)
    feats = normal_values(splits[0], (SCENE_TILES, SEQ, D), 1.0, 6.0, ((0, 4), (1, 8)))
    face_rows = with_ends(jax.random.randint(splits[1], (SCENE_TILES, N_CTX * FACE), 0, VOX_DEV), jax.random.fold_in(splits[1], 1), 0, VOX_DEV - 1).astype(jnp.int32)
    neighbours = draw_neighbours(jax.random.fold_in(splits[12], 71), 0)
    block_len = draw_block_len(jax.random.fold_in(splits[12], 71), 0)
    dilated = draw_dilated(jax.random.fold_in(splits[12], 71), 0)
    pick = with_ends(jax.random.randint(splits[5], (SCENE_TILES, N_CTX, N_CTX), 0, RANGE_BLOCKS), jax.random.fold_in(splits[5], 1), 0, RANGE_BLOCKS - 1).astype(jnp.int32)
    cpe_weight = normal_values(splits[6], (7, D, D), (7 * D) ** -0.5, 0.125)
    cpe_bias = normal_values(splits[7], (D,), 0.5, 3.0, (), jnp.float32)
    ln_gain = jnp.clip(1.0 + 0.18 * jax.random.normal(splits[8], (D,), jnp.float32), 0.1, 1.9)
    ln_bias = normal_values(splits[9], (D,), 0.5, 3.0, (), jnp.float32)
    w_qkv = draw_w_qkv(jax.random.fold_in(splits[12], 71), 0)
    w_out = normal_values(splits[11], (D, D), (max(D // 64, 1)) ** -0.5, 3.0)
    return dict(feats=feats, face_rows=face_rows, neighbours=neighbours, block_len=block_len, dilated=dilated, pick=pick, cpe_weight=cpe_weight, cpe_bias=cpe_bias, ln_gain=ln_gain, ln_bias=ln_bias, w_qkv=w_qkv, w_out=w_out)


def layer_norm(hidden, ln_gain, ln_bias):
    center = hidden - lax.optimization_barrier(jnp.mean(hidden, axis=-1, keepdims=True))
    variance = lax.optimization_barrier(jnp.mean(center * center, axis=-1, keepdims=True))
    return (center * lax.rsqrt(variance + 1e-05) * ln_gain + ln_bias).astype(jnp.bfloat16)

def attend(query_blk, key_rows, value_rows, valid_keys):
    rows_q = query_blk.shape[0]
    head_dim = D // HEADS
    query_heads = query_blk.astype(jnp.float32).reshape(rows_q, HEADS, head_dim)
    key_heads = key_rows.astype(jnp.float32).reshape(-1, HEADS, head_dim)
    value_heads = value_rows.astype(jnp.float32).reshape(-1, HEADS, head_dim)
    scores = jnp.einsum('qhd,khd->hqk', query_heads, key_heads) * (1.0 / math.sqrt(head_dim))
    scores = jnp.where(valid_keys[None, None, :], scores, -1e+30)
    row_peak = lax.optimization_barrier(jnp.max(scores, axis=-1, keepdims=True))
    raw_weights = jnp.exp(scores - row_peak)
    denominator = lax.optimization_barrier(jnp.sum(raw_weights, axis=-1, keepdims=True))
    attn_weights = (raw_weights / denominator).astype(jnp.bfloat16)
    mixed_heads = jnp.einsum('hqk,khd->qhd', attn_weights.astype(jnp.float32), value_heads)
    return mixed_heads.reshape(rows_q, D).astype(jnp.bfloat16)

def as_index(value):
    return jnp.asarray(value).astype(jnp.int32)

def reference(feats, face_rows, neighbours, block_len, dilated, pick, cpe_weight, cpe_bias, ln_gain, ln_bias, w_qkv, w_out):
    seq_len = VOX_DEV * N_CTX
    zero_index = as_index(0)
    per_range = feats.reshape(N_SPACE, N_CTX, VOX_DEV, D)
    face_ids = face_rows.reshape(N_SPACE, N_CTX, FACE)
    faces = jax.vmap(jax.vmap(lambda rows_all, picked: rows_all[picked]))(per_range, face_ids)
    empty_face = jnp.zeros((1, N_CTX, FACE, D), feats.dtype)
    faces_pad = jnp.concatenate([empty_face, faces, empty_face], 0)
    feats_pad = jnp.pad(feats, ((0, 0), (EDGE, EDGE), (0, 0)))

    def encode(index):
        tile = as_index(index // N_CTX)
        range_id = as_index(index % N_CTX)
        row_start = as_index(range_id * VOX_DEV)
        edge_rows = lax.dynamic_slice(feats_pad, (tile, row_start, zero_index), (1, VOX_DEV + 2 * EDGE, D))[0]
        face_block = lax.dynamic_slice(faces_pad, (tile, range_id, zero_index, zero_index), (3, 1, FACE, D)).reshape(3 * FACE, D)
        neighbour_table = jnp.concatenate([edge_rows, face_block, jnp.zeros((1, D), feats.dtype)], 0)
        table_ids = lax.dynamic_slice(neighbours, (tile, row_start, zero_index), (1, VOX_DEV, 6))[0]
        own_rows = edge_rows[EDGE:EDGE + VOX_DEV]
        conv_out = jnp.dot(own_rows, cpe_weight[0], preferred_element_type=jnp.float32)
        for offset in range(6):
            conv_out = conv_out + jnp.dot(neighbour_table[table_ids[:, offset]], cpe_weight[offset + 1], preferred_element_type=jnp.float32)
        hidden = own_rows.astype(jnp.float32) + conv_out + cpe_bias
        normed = layer_norm(hidden, ln_gain, ln_bias)
        projected = jnp.dot(normed, w_qkv, preferred_element_type=jnp.float32)
        return (hidden, projected[:, :D].astype(jnp.bfloat16), projected[:, D:2 * D].astype(jnp.bfloat16), projected[:, 2 * D:].astype(jnp.bfloat16))
    hidden, queries, keys_all, values_all = lax.map(encode, jnp.arange(N_SPACE * N_CTX, dtype=jnp.int32))
    hidden = hidden.reshape(N_SPACE, seq_len, D)
    queries = queries.reshape(N_SPACE, seq_len, D)
    keys_all = keys_all.reshape(N_SPACE, seq_len, D)
    values_all = values_all.reshape(N_SPACE, seq_len, D)
    blocks_dev = VOX_DEV // BLK
    blocks_tile = blocks_dev * N_CTX
    keys_pad = jnp.pad(keys_all, ((0, 0), (BLK, BLK), (0, 0)))
    values_pad = jnp.pad(values_all, ((0, 0), (BLK, BLK), (0, 0)))
    lens_ext = jnp.pad(block_len, ((0, 0), (1, 1)))
    positions = jnp.arange(BLK, dtype=jnp.int32)

    def attend_block(index):
        tile = as_index(index // blocks_tile)
        block = as_index(index % blocks_tile)
        range_id = as_index(block // blocks_dev)
        row_start = as_index(block * BLK)
        query_blk = lax.dynamic_slice(queries, (tile, row_start, zero_index), (1, BLK, D))[0]
        window_keys = lax.dynamic_slice(keys_pad, (tile, row_start, zero_index), (1, 3 * BLK, D))[0]
        window_values = lax.dynamic_slice(values_pad, (tile, row_start, zero_index), (1, 3 * BLK, D))[0]
        win_lens = lax.dynamic_slice(lens_ext, (tile, block), (1, 3))[0]
        slot_ids = dilated[tile, block]
        far_ids = as_index(slot_ids * blocks_dev + pick[tile, slot_ids, range_id])
        row_ids = as_index((far_ids[:, None] * BLK + positions[None, :]).reshape(-1))
        remote_keys = keys_all[tile, row_ids]
        remote_values = values_all[tile, row_ids]
        far_lens = block_len[tile, far_ids]
        lens_row = jnp.concatenate([win_lens, far_lens], 0)
        valid_keys = (positions[None, :] < lens_row[:, None]).reshape(-1)
        attended = attend(query_blk, jnp.concatenate([window_keys, remote_keys], 0), jnp.concatenate([window_values, remote_values], 0), valid_keys)
        hidden_block = lax.dynamic_slice(hidden, (tile, row_start, zero_index), (1, BLK, D))[0]
        return (hidden_block + jnp.dot(attended, w_out, preferred_element_type=jnp.float32)).astype(jnp.bfloat16)
    output = lax.map(attend_block, jnp.arange(N_SPACE * blocks_tile, dtype=jnp.int32))
    return output.reshape(N_SPACE, seq_len, D)
```

```python
import math

import jax
import jax.numpy as jnp
from jax import lax
from jax.experimental import pallas as pl
from jax.experimental.pallas import tpu as pltpu
from jax.sharding import PartitionSpec as P

D = 256
HEADS = 8
BLK = 128
EDGE = 128
FACE = 256


def extended(block, sides, width):
    for axis, dim in sides:
        count = lax.axis_size(axis)
        forward = [(i, i + 1) for i in range(count - 1)]
        backward = [(target, source) for source, target in forward]
        low = lax.ppermute(
            lax.slice_in_dim(block, block.shape[dim] - width, None, axis=dim), axis, forward
        )
        high = lax.ppermute(lax.slice_in_dim(block, 0, width, axis=dim), axis, backward)
        block = jnp.concatenate([low, block, high], axis=dim)
    return block


ROWS = 256


def encode_kernel(
    ids_ref, own_ref, table_ref, weight_ref, bias_ref, gain_ref, shift_ref, qkv_ref,
    hidden_ref, query_ref, kv_ref,
):
    rows = own_ref.shape[0]
    count = table_ref.shape[0]
    own = own_ref[...]
    conv = jnp.dot(own, weight_ref[0], preferred_element_type=jnp.float32)
    lane = lax.broadcasted_iota(jnp.int32, (rows, 128), 1)
    ids = ids_ref[...]
    for offset in range(6):
        column = jnp.broadcast_to(ids[:, offset : offset + 1], (rows, 128))
        low = column & 127
        high = (column >> 7).astype(jnp.float32).astype(jnp.bfloat16)
        hot = jnp.where(low == lane, 1.0, 0.0).astype(jnp.bfloat16)
        zero = jnp.zeros_like(hot)
        chosen = jnp.concatenate(
            [jnp.where(high == jnp.bfloat16(part), hot, zero) for part in range(count // 128)], 1
        )
        picked = jnp.dot(chosen, table_ref[...], preferred_element_type=jnp.float32)
        conv = conv + jnp.dot(
            picked.astype(jnp.bfloat16), weight_ref[offset + 1], preferred_element_type=jnp.float32
        )
    hidden = own.astype(jnp.float32) + conv + bias_ref[...]
    hidden_ref[...] = hidden
    center = hidden - jnp.mean(hidden, axis=-1, keepdims=True)
    variance = jnp.mean(center * center, axis=-1, keepdims=True)
    normed = (center * lax.rsqrt(variance + 1e-05) * gain_ref[...] + shift_ref[...]).astype(jnp.bfloat16)
    projected = jnp.dot(normed, qkv_ref[...], preferred_element_type=jnp.float32).astype(jnp.bfloat16)
    query_ref[...] = projected[:, :D]
    kv_ref[...] = projected[:, D:]


def encode(ids, own, table, weight, bias, gain, shift, w_qkv):
    count, width = own.shape
    whole = lambda shape: pl.BlockSpec(shape, lambda i: (0,) * len(shape))
    tile = lambda cols: pl.BlockSpec((ROWS, cols), lambda i: (i, 0))
    return pl.pallas_call(
        encode_kernel,
        grid=(count // ROWS,),
        in_specs=[
            tile(6), tile(width), whole(table.shape), whole(weight.shape),
            whole((1, width)), whole((1, width)), whole((1, width)), whole(w_qkv.shape),
        ],
        out_specs=[tile(width), tile(width), tile(2 * width)],
        out_shape=[
            jax.ShapeDtypeStruct((count, width), jnp.float32),
            jax.ShapeDtypeStruct((count, width), jnp.bfloat16),
            jax.ShapeDtypeStruct((count, 2 * width), jnp.bfloat16),
        ],
        compiler_params=pltpu.CompilerParams(vmem_limit_bytes=40 * 2**20),
    )(ids, own, table, weight, bias[None], gain[None], shift[None], w_qkv)


GROUP = 4


def attend_kernel(
    slots_ref, lens_ref, query_ref, window_ref, remote_ref, hidden_ref, out_w_ref, out_ref, kv_ref
):
    blk = pl.program_id(0)
    start = pl.multiple_of(blk * BLK, BLK)
    kv_ref[0 : 3 * BLK, :] = window_ref[pl.ds(start, 3 * BLK), :]
    for slot in range(4):
        where = pl.multiple_of(slots_ref[blk, slot] * BLK, BLK)
        kv_ref[(3 + slot) * BLK : (4 + slot) * BLK, :] = remote_ref[pl.ds(where, BLK), :]
    lane = lax.broadcasted_iota(jnp.int32, (1, BLK), 1)
    mask = jnp.concatenate(
        [jnp.where(lane < lens_ref[blk, part], 0.0, -1e30) for part in range(7)], 1
    )
    head_dim = D // HEADS
    head_of = lax.broadcasted_iota(jnp.int32, (BLK, D), 1) // head_dim
    query = query_ref[...]
    keys = kv_ref[:, :D]
    values = kv_ref[:, D:]
    scale = 1.0 / math.sqrt(head_dim)
    attended = jnp.zeros((BLK, D), jnp.float32)
    for group in range(0, HEADS, GROUP):
        stacked = jnp.concatenate(
            [jnp.where(head_of == head, query, jnp.zeros_like(query)) for head in range(group, group + GROUP)], 0
        )
        scores = lax.dot_general(
            stacked, keys, (((1,), (1,)), ((), ())), preferred_element_type=jnp.float32
        ) * scale + mask
        raw = jnp.exp(scores - jnp.max(scores, axis=-1, keepdims=True))
        inverse = 1.0 / jnp.sum(raw, axis=-1, keepdims=True)
        weights = (raw * inverse).astype(jnp.bfloat16)
        mixed = jnp.dot(weights, values, preferred_element_type=jnp.float32)
        for part in range(GROUP):
            attended = jnp.where(head_of == group + part, mixed[part * BLK : (part + 1) * BLK], attended)
    out = hidden_ref[...] + jnp.dot(
        attended.astype(jnp.bfloat16), out_w_ref[...], preferred_element_type=jnp.float32
    )
    out_ref[...] = out.astype(jnp.bfloat16)


def attend(slots, lens, queries, window, remote, hidden, w_out):
    count, width = queries.shape
    whole = lambda shape: pl.BlockSpec(shape, lambda i, *_: (0,) * len(shape))
    tile = pl.BlockSpec((BLK, width), lambda i, *_: (i, 0))
    return pl.pallas_call(
        attend_kernel,
        grid_spec=pltpu.PrefetchScalarGridSpec(
            num_scalar_prefetch=2,
            grid=(count // BLK,),
            in_specs=[tile, whole(window.shape), whole(remote.shape), tile, whole(w_out.shape)],
            out_specs=tile,
            scratch_shapes=[pltpu.VMEM((7 * BLK, 2 * width), jnp.bfloat16)],
        ),
        out_shape=jax.ShapeDtypeStruct((count, width), jnp.bfloat16),
        compiler_params=pltpu.CompilerParams(vmem_limit_bytes=48 * 2**20),
    )(slots, lens, queries, window, remote, hidden, w_out)


def on_device(
    feats,
    face_rows,
    neighbours,
    block_len,
    dilated,
    pick,
    cpe_weight,
    cpe_bias,
    ln_gain,
    ln_bias,
    w_qkv,
    w_out,
):
    voxels = feats[0]
    count_vox = voxels.shape[0]
    feat_width = voxels.shape[1]
    blocks_dev = count_vox // BLK
    my_range = lax.axis_index("ctx")
    edge_rows = extended(voxels, (("ctx", 0),), EDGE)
    face_out = voxels[face_rows[0]]
    face_all = extended(face_out, (("space", 0),), FACE)
    neighbour_table = jnp.concatenate([edge_rows, face_all], 0)
    hidden, queries, key_value = encode(
        neighbours[0], voxels, neighbour_table, cpe_weight, cpe_bias, ln_gain, ln_bias, w_qkv
    )
    window_kv = extended(key_value, (("ctx", 0),), BLK)
    pick_tile = pick[0]
    send_index = pick_tile[my_range]
    recv_index = pick_tile[:, my_range]
    outgoing = key_value.reshape(blocks_dev, BLK, 2 * feat_width)[send_index]
    remote_kv = lax.all_to_all(outgoing, "ctx", split_axis=0, concat_axis=0, tiled=True)
    lens_tile = block_len[0]
    lens_ext = jnp.pad(lens_tile, (1, 1))
    local_ids = jnp.arange(blocks_dev, dtype=jnp.int32)
    global_ids = my_range * blocks_dev + local_ids
    win_lens = lens_ext[global_ids[:, None] + jnp.arange(3, dtype=jnp.int32)[None, :]]
    slot_ids = dilated[0]
    far_ids = slot_ids * blocks_dev + recv_index[slot_ids]
    far_lens = lens_tile[far_ids]
    key_lens = jnp.concatenate([win_lens, far_lens], 1)
    output = attend(
        slot_ids, key_lens, queries, window_kv, remote_kv.reshape(-1, 2 * feat_width), hidden, w_out
    )
    return output[None]


def solution(mesh):
    placed = (
        P("space", "ctx", None),
        P("space", "ctx"),
        P("space", "ctx", None),
        P("space", None),
        P("space", "ctx", None),
        P("space", None, None),
        P(),
        P(),
        P(),
        P(),
        P(),
        P(),
    )
    return jax.shard_map(
        on_device, mesh=mesh, in_specs=placed, out_specs=P("space", "ctx", None), check_vma=False
    )
```

```python
import functools
import math

import jax
import jax.numpy as jnp
from jax import lax
from jax.experimental import pallas as pl
from jax.experimental.pallas import tpu as pltpu
from jax.sharding import PartitionSpec as P

D = 256
HEADS = 8
BLK = 128
EDGE = 128
FACE = 256


MESH = pl.DeviceIdType.MESH


def table_kernel(n_space, n_ctx, rows_ref, own_ref, table_ref, face_ref, send_sem, recv_sem):
    space, ctx = lax.axis_index("space"), lax.axis_index("ctx")
    count = own_ref.shape[0]
    base = count + 2 * EDGE
    sides = (
        (ctx < n_ctx - 1, ctx > 0, (space, ctx + 1)),
        (ctx > 0, ctx < n_ctx - 1, (space, ctx - 1)),
        (space < n_space - 1, space > 0, (space + 1, ctx)),
        (space > 0, space < n_space - 1, (space - 1, ctx)),
    )
    barrier = pltpu.get_barrier_semaphore()
    for there, _, peer in sides:
        @pl.when(there)
        def _():
            pl.semaphore_signal(barrier, inc=1, device_id=peer, device_id_type=MESH)
    pl.semaphore_wait(barrier, sum(there.astype(jnp.int32) for there, _, _ in sides))
    targets = (
        (0, EDGE), (EDGE + count, EDGE), (base, FACE), (base + 2 * FACE, FACE)
    )
    sources = (
        own_ref.at[pl.ds(count - EDGE, EDGE)], own_ref.at[pl.ds(0, EDGE)], face_ref, face_ref
    )
    copies = [
        pltpu.make_async_remote_copy(
            src_ref=sources[i],
            dst_ref=table_ref.at[pl.ds(*targets[i])],
            send_sem=send_sem.at[i],
            recv_sem=recv_sem.at[i],
            device_id=sides[i][2],
            device_id_type=MESH,
        )
        for i in range(4)
    ]
    for i in (0, 1):
        pl.when(sides[i][0])(copies[i].start)
    place = lax.broadcasted_iota(jnp.int32, (FACE, count), 1)
    hot = jnp.where(rows_ref[...] == place, 1.0, 0.0).astype(jnp.bfloat16)
    face = jnp.dot(hot, own_ref[...], preferred_element_type=jnp.float32).astype(jnp.bfloat16)
    face_ref[...] = face
    for i in (2, 3):
        pl.when(sides[i][0])(copies[i].start)
    table_ref[EDGE : EDGE + count, :] = own_ref[...]
    table_ref[base + FACE : base + 2 * FACE, :] = face
    for i in range(4):
        first, width = targets[i]

        @pl.when(jnp.logical_not(sides[i][1]))
        def _():
            table_ref[first : first + width, :] = jnp.zeros((width, D), jnp.bfloat16)
    for i in range(4):
        pl.when(sides[i][0])(copies[i].wait_send)
        pl.when(sides[i][1])(copies[i].wait_recv)


def build_table(rows, own, n_space, n_ctx):
    count, width = own.shape
    vmem = pl.BlockSpec(memory_space=pltpu.VMEM)
    return pl.pallas_call(
        functools.partial(table_kernel, n_space, n_ctx),
        in_specs=[vmem, vmem],
        out_specs=vmem,
        out_shape=jax.ShapeDtypeStruct((count + 2 * EDGE + 3 * FACE, width), own.dtype),
        scratch_shapes=[
            pltpu.VMEM((FACE, width), own.dtype),
            pltpu.SemaphoreType.DMA((4,)),
            pltpu.SemaphoreType.DMA((4,)),
        ],
        compiler_params=pltpu.CompilerParams(
            collective_id=0, has_side_effects=True, vmem_limit_bytes=24 * 2**20
        ),
    )(rows[:, None], own)


def exchange_kernel(n_ctx, out_ref, ends_ref, far_ref, send_sem, recv_sem, local_sem):
    space, ctx = lax.axis_index("space"), lax.axis_index("ctx")
    barrier = pltpu.get_barrier_semaphore()
    for step in range(1, n_ctx):
        peer = lax.rem(ctx + step, n_ctx)
        pl.semaphore_signal(barrier, inc=1, device_id=(space, peer), device_id_type=MESH)
    pl.semaphore_wait(barrier, n_ctx - 1)
    copies = []
    for step in range(1, n_ctx):
        peer = lax.rem(ctx + step, n_ctx)
        copies.append(
            pltpu.make_async_remote_copy(
                src_ref=out_ref.at[peer],
                dst_ref=far_ref.at[ctx],
                send_sem=send_sem.at[step],
                recv_sem=recv_sem.at[step],
                device_id=(space, peer),
                device_id_type=MESH,
            )
        )
    sides = (
        (ctx < n_ctx - 1, ctx > 0, ctx + 1, 1, n_ctx),
        (ctx > 0, ctx < n_ctx - 1, ctx - 1, 0, n_ctx + 1),
    )
    edges = [
        pltpu.make_async_remote_copy(
            src_ref=ends_ref.at[source],
            dst_ref=far_ref.at[slot],
            send_sem=send_sem.at[slot],
            recv_sem=recv_sem.at[slot],
            device_id=(space, peer),
            device_id_type=MESH,
        )
        for _, _, peer, source, slot in sides
    ]
    order = sorted(range(1, n_ctx), key=lambda step: abs(step - n_ctx // 2))
    for step in order:
        copies[step - 1].start()
    for side, edge in zip(sides, edges):
        pl.when(side[0])(edge.start)
    own = pltpu.make_async_copy(out_ref.at[ctx], far_ref.at[ctx], local_sem)
    own.start()
    for side in sides:
        @pl.when(jnp.logical_not(side[1]))
        def _():
            far_ref[side[4]] = jnp.zeros(far_ref.shape[1:], jnp.bfloat16)
    own.wait()
    for copy in copies:
        copy.wait()
    for side, edge in zip(sides, edges):
        pl.when(side[0])(edge.wait_send)
        pl.when(side[1])(edge.wait_recv)


def exchange(outgoing, ends, n_ctx):
    vmem = pl.BlockSpec(memory_space=pltpu.VMEM)
    return pl.pallas_call(
        functools.partial(exchange_kernel, n_ctx),
        in_specs=[vmem, vmem],
        out_specs=vmem,
        out_shape=jax.ShapeDtypeStruct((n_ctx + 2,) + outgoing.shape[1:], outgoing.dtype),
        scratch_shapes=[
            pltpu.SemaphoreType.DMA((n_ctx + 2,)),
            pltpu.SemaphoreType.DMA((n_ctx + 2,)),
            pltpu.SemaphoreType.DMA,
        ],
        compiler_params=pltpu.CompilerParams(
            collective_id=1, has_side_effects=True, vmem_limit_bytes=24 * 2**20
        ),
    )(outgoing, ends)


ROWS = 256


def encode_kernel(
    pick_ref, ids_ref, own_ref, table_ref, weight_ref, bias_ref, gain_ref, shift_ref, qkv_ref,
    hidden_ref, query_ref, kv_ref, outgoing_ref, ends_ref, normed_ref,
):
    rows = own_ref.shape[0]
    count = table_ref.shape[0]
    own = own_ref[...]
    conv = jnp.dot(own, weight_ref[0], preferred_element_type=jnp.float32)
    lane = lax.broadcasted_iota(jnp.int32, (rows, 128), 1)
    ids = ids_ref[...]
    for offset in range(6):
        column = jnp.broadcast_to(ids[:, offset : offset + 1], (rows, 128))
        low = column & 127
        high = (column >> 7).astype(jnp.float32).astype(jnp.bfloat16)
        hot = jnp.where(low == lane, 1.0, 0.0).astype(jnp.bfloat16)
        zero = jnp.zeros_like(hot)
        chosen = jnp.concatenate(
            [jnp.where(high == jnp.bfloat16(part), hot, zero) for part in range(count // 128)], 1
        )
        picked = jnp.dot(chosen, table_ref[...], preferred_element_type=jnp.float32)
        conv = conv + jnp.dot(
            picked.astype(jnp.bfloat16), weight_ref[offset + 1], preferred_element_type=jnp.float32
        )
    hidden = own.astype(jnp.float32) + conv + bias_ref[...]
    hidden_ref[...] = hidden
    center = hidden - jnp.mean(hidden, axis=-1, keepdims=True)
    variance = jnp.mean(center * center, axis=-1, keepdims=True)
    normed = (center * lax.rsqrt(variance + 1e-05) * gain_ref[...] + shift_ref[...]).astype(jnp.bfloat16)
    projected = jnp.dot(normed, qkv_ref[...], preferred_element_type=jnp.float32).astype(jnp.bfloat16)
    query_ref[...] = projected[:, :D]
    kv_ref[...] = projected[:, D:]
    step = pl.program_id(0)
    normed_ref[pl.ds(pl.multiple_of(step * rows, rows), rows), :] = normed

    @pl.when(step == pl.num_programs(0) - 1)
    def _():
        ends_ref[0] = normed_ref[:BLK, :]
        ends_ref[1] = normed_ref[normed_ref.shape[0] - BLK :, :]
        for peer in range(outgoing_ref.shape[0]):
            first = pl.multiple_of(pick_ref[lax.axis_index("ctx"), peer] * BLK, BLK)
            outgoing_ref[peer] = normed_ref[pl.ds(first, BLK), :]


def encode(pick, ids, own, table, weight, bias, gain, shift, w_qkv):
    count, width = own.shape
    whole = lambda shape: pl.BlockSpec(shape, lambda i, *_: (0,) * len(shape))
    tile = lambda cols: pl.BlockSpec((ROWS, cols), lambda i, *_: (i, 0))
    peers = pick.shape[0]
    return pl.pallas_call(
        encode_kernel,
        grid_spec=pltpu.PrefetchScalarGridSpec(
            num_scalar_prefetch=1,
            grid=(count // ROWS,),
            in_specs=[
                tile(6), tile(width), whole(table.shape), whole(weight.shape),
                whole((1, width)), whole((1, width)), whole((1, width)), whole(w_qkv.shape),
            ],
            out_specs=[
                tile(width), tile(width), tile(2 * width),
                whole((peers, BLK, width)), whole((2, BLK, width)),
            ],
            scratch_shapes=[pltpu.VMEM((count, width), jnp.bfloat16)],
        ),
        out_shape=[
            jax.ShapeDtypeStruct((count, width), jnp.float32),
            jax.ShapeDtypeStruct((count, width), jnp.bfloat16),
            jax.ShapeDtypeStruct((count, 2 * width), jnp.bfloat16),
            jax.ShapeDtypeStruct((peers, BLK, width), jnp.bfloat16),
            jax.ShapeDtypeStruct((2, BLK, width), jnp.bfloat16),
        ],
        compiler_params=pltpu.CompilerParams(vmem_limit_bytes=40 * 2**20),
    )(pick, ids, own, table, weight, bias[None], gain[None], shift[None], w_qkv)


GROUP = 4


def attend_kernel(
    slots_ref, lens_ref, pick_ref, query_ref, near_ref, far_ref, qkv_ref, hidden_ref, out_w_ref,
    out_ref, far_kv_ref, window_ref, kv_ref,
):
    blk = pl.program_id(0)
    peers = pick_ref.shape[0]
    count = near_ref.shape[0]
    blocks = count // BLK
    ctx = lax.axis_index("ctx")

    @pl.when(blk == 0)
    def _():
        kv_weight = qkv_ref[:, D:]
        for peer in range(peers):
            far_kv_ref[peer * BLK : (peer + 1) * BLK, :] = jnp.dot(
                far_ref[peer], kv_weight, preferred_element_type=jnp.float32
            ).astype(jnp.bfloat16)
        window_ref[BLK : BLK + count, :] = near_ref[...]
        for side, first in ((peers, 0), (peers + 1, BLK + count)):
            window_ref[first : first + BLK, :] = jnp.dot(
                far_ref[side], kv_weight, preferred_element_type=jnp.float32
            ).astype(jnp.bfloat16)

    start = pl.multiple_of(blk * BLK, BLK)
    kv_ref[0 : 3 * BLK, :] = window_ref[pl.ds(start, 3 * BLK), :]
    lens = []
    for part in range(3):
        block = ctx * blocks + blk + part - 1
        inside = jnp.logical_and(block >= 0, block < peers * blocks)
        lens.append(jnp.where(inside, lens_ref[jnp.clip(block, 0, peers * blocks - 1)], 0))
    for slot in range(4):
        source = slots_ref[blk, slot]
        lens.append(lens_ref[source * blocks + pick_ref[source, ctx]])
        where = pl.multiple_of(source * BLK, BLK)
        kv_ref[(3 + slot) * BLK : (4 + slot) * BLK, :] = far_kv_ref[pl.ds(where, BLK), :]
    lane = lax.broadcasted_iota(jnp.int32, (1, BLK), 1)
    mask = jnp.concatenate([jnp.where(lane < valid, 0.0, -1e30) for valid in lens], 1)
    head_dim = D // HEADS
    head_of = lax.broadcasted_iota(jnp.int32, (BLK, D), 1) // head_dim
    query = query_ref[...]
    keys = kv_ref[:, :D]
    values = kv_ref[:, D:]
    scale = 1.0 / math.sqrt(head_dim)
    attended = jnp.zeros((BLK, D), jnp.float32)
    for group in range(0, HEADS, GROUP):
        stacked = jnp.concatenate(
            [jnp.where(head_of == head, query, jnp.zeros_like(query)) for head in range(group, group + GROUP)], 0
        )
        scores = lax.dot_general(
            stacked, keys, (((1,), (1,)), ((), ())), preferred_element_type=jnp.float32
        ) * scale + mask
        raw = jnp.exp(scores - jnp.max(scores, axis=-1, keepdims=True))
        inverse = 1.0 / jnp.sum(raw, axis=-1, keepdims=True)
        weights = (raw * inverse).astype(jnp.bfloat16)
        mixed = jnp.dot(weights, values, preferred_element_type=jnp.float32)
        for part in range(GROUP):
            attended = jnp.where(head_of == group + part, mixed[part * BLK : (part + 1) * BLK], attended)
    out = hidden_ref[...] + jnp.dot(
        attended.astype(jnp.bfloat16), out_w_ref[...], preferred_element_type=jnp.float32
    )
    out_ref[...] = out.astype(jnp.bfloat16)


def attend(slots, lens, pick, queries, near, far, w_qkv, hidden, w_out):
    count, width = queries.shape
    whole = lambda shape: pl.BlockSpec(shape, lambda i, *_: (0,) * len(shape))
    tile = pl.BlockSpec((BLK, width), lambda i, *_: (i, 0))
    return pl.pallas_call(
        attend_kernel,
        grid_spec=pltpu.PrefetchScalarGridSpec(
            num_scalar_prefetch=3,
            grid=(count // BLK,),
            in_specs=[
                tile, whole(near.shape), whole(far.shape), whole(w_qkv.shape), tile, whole(w_out.shape)
            ],
            out_specs=tile,
            scratch_shapes=[
                pltpu.VMEM((pick.shape[0] * BLK, 2 * width), jnp.bfloat16),
                pltpu.VMEM((count + 2 * BLK, 2 * width), jnp.bfloat16),
                pltpu.VMEM((7 * BLK, 2 * width), jnp.bfloat16),
            ],
        ),
        out_shape=jax.ShapeDtypeStruct((count, width), jnp.bfloat16),
        compiler_params=pltpu.CompilerParams(vmem_limit_bytes=48 * 2**20),
    )(slots, lens, pick, queries, near, far, w_qkv, hidden, w_out)


def on_device(
    feats,
    face_rows,
    neighbours,
    block_len,
    dilated,
    pick,
    cpe_weight,
    cpe_bias,
    ln_gain,
    ln_bias,
    w_qkv,
    w_out,
):
    voxels = feats[0]
    n_space, n_ctx = lax.axis_size("space"), lax.axis_size("ctx")
    table = build_table(face_rows[0], voxels, n_space, n_ctx)
    hidden, queries, near, outgoing, ends = encode(
        pick[0], neighbours[0], voxels, table, cpe_weight, cpe_bias, ln_gain, ln_bias, w_qkv
    )
    far = exchange(outgoing, ends, n_ctx)
    return attend(dilated[0], block_len[0], pick[0], queries, near, far, w_qkv, hidden, w_out)[None]


def solution(mesh):
    placed = (
        P("space", "ctx", None),
        P("space", "ctx"),
        P("space", "ctx", None),
        P("space", None),
        P("space", "ctx", None),
        P("space", None, None),
        P(),
        P(),
        P(),
        P(),
        P(),
        P(),
    )
    return jax.shard_map(
        on_device, mesh=mesh, in_specs=placed, out_specs=P("space", "ctx", None), check_vma=False
    )
```

```python
import functools
import math

import jax
import jax.numpy as jnp
from jax import lax
from jax.experimental import pallas as pl
from jax.experimental.pallas import tpu as pltpu
from jax.sharding import PartitionSpec as P

D = 256
HEADS = 8
BLK = 128
EDGE = 128
FACE = 256


MESH = pl.DeviceIdType.MESH


def table_kernel(n_space, n_ctx, rows_ref, own_ref, table_ref, face_ref, send_sem, recv_sem):
    space, ctx = lax.axis_index("space"), lax.axis_index("ctx")
    count = own_ref.shape[0]
    base = count + 2 * EDGE
    sides = (
        (ctx < n_ctx - 1, ctx > 0, (space, ctx + 1)),
        (ctx > 0, ctx < n_ctx - 1, (space, ctx - 1)),
        (space < n_space - 1, space > 0, (space + 1, ctx)),
        (space > 0, space < n_space - 1, (space - 1, ctx)),
    )
    barrier = pltpu.get_barrier_semaphore()
    for there, _, peer in sides:
        @pl.when(there)
        def _():
            pl.semaphore_signal(barrier, inc=1, device_id=peer, device_id_type=MESH)
    pl.semaphore_wait(barrier, sum(there.astype(jnp.int32) for there, _, _ in sides))
    targets = (
        (0, EDGE), (EDGE + count, EDGE), (base, FACE), (base + 2 * FACE, FACE)
    )
    sources = (
        own_ref.at[pl.ds(count - EDGE, EDGE)], own_ref.at[pl.ds(0, EDGE)], face_ref, face_ref
    )
    copies = [
        pltpu.make_async_remote_copy(
            src_ref=sources[i],
            dst_ref=table_ref.at[pl.ds(*targets[i])],
            send_sem=send_sem.at[i],
            recv_sem=recv_sem.at[i],
            device_id=sides[i][2],
            device_id_type=MESH,
        )
        for i in range(4)
    ]
    for i in (0, 1):
        pl.when(sides[i][0])(copies[i].start)
    place = lax.broadcasted_iota(jnp.int32, (FACE, count), 1)
    hot = jnp.where(rows_ref[...] == place, 1.0, 0.0).astype(jnp.bfloat16)
    face = jnp.dot(hot, own_ref[...], preferred_element_type=jnp.float32).astype(jnp.bfloat16)
    face_ref[...] = face
    for i in (2, 3):
        pl.when(sides[i][0])(copies[i].start)
    table_ref[EDGE : EDGE + count, :] = own_ref[...]
    table_ref[base + FACE : base + 2 * FACE, :] = face
    for i in range(4):
        first, width = targets[i]

        @pl.when(jnp.logical_not(sides[i][1]))
        def _():
            table_ref[first : first + width, :] = jnp.zeros((width, D), jnp.bfloat16)
    for i in range(4):
        pl.when(sides[i][0])(copies[i].wait_send)
        pl.when(sides[i][1])(copies[i].wait_recv)


def build_table(rows, own, n_space, n_ctx):
    count, width = own.shape
    vmem = pl.BlockSpec(memory_space=pltpu.VMEM)
    return pl.pallas_call(
        functools.partial(table_kernel, n_space, n_ctx),
        in_specs=[vmem, vmem],
        out_specs=vmem,
        out_shape=jax.ShapeDtypeStruct((count + 2 * EDGE + 3 * FACE, width), own.dtype),
        scratch_shapes=[
            pltpu.VMEM((FACE, width), own.dtype),
            pltpu.SemaphoreType.DMA((4,)),
            pltpu.SemaphoreType.DMA((4,)),
        ],
        compiler_params=pltpu.CompilerParams(
            collective_id=0, has_side_effects=True, vmem_limit_bytes=8 * 2**20
        ),
    )(rows[:, None], own)


def exchange_kernel(n_ctx, out_ref, ends_ref, far_ref, send_sem, recv_sem, local_sem):
    space, ctx = lax.axis_index("space"), lax.axis_index("ctx")
    barrier = pltpu.get_barrier_semaphore()
    for step in range(1, n_ctx):
        peer = lax.rem(ctx + step, n_ctx)
        pl.semaphore_signal(barrier, inc=1, device_id=(space, peer), device_id_type=MESH)
    pl.semaphore_wait(barrier, n_ctx - 1)
    copies = []
    for step in range(1, n_ctx):
        peer = lax.rem(ctx + step, n_ctx)
        copies.append(
            pltpu.make_async_remote_copy(
                src_ref=out_ref.at[peer],
                dst_ref=far_ref.at[ctx],
                send_sem=send_sem.at[step],
                recv_sem=recv_sem.at[step],
                device_id=(space, peer),
                device_id_type=MESH,
            )
        )
    sides = (
        (ctx < n_ctx - 1, ctx > 0, ctx + 1, 1, n_ctx),
        (ctx > 0, ctx < n_ctx - 1, ctx - 1, 0, n_ctx + 1),
    )
    edges = [
        pltpu.make_async_remote_copy(
            src_ref=ends_ref.at[source],
            dst_ref=far_ref.at[slot],
            send_sem=send_sem.at[slot],
            recv_sem=recv_sem.at[slot],
            device_id=(space, peer),
            device_id_type=MESH,
        )
        for _, _, peer, source, slot in sides
    ]
    order = sorted(range(1, n_ctx), key=lambda step: abs(step - n_ctx // 2))
    for step in order:
        copies[step - 1].start()
    for side, edge in zip(sides, edges):
        pl.when(side[0])(edge.start)
    own = pltpu.make_async_copy(out_ref.at[ctx], far_ref.at[ctx], local_sem)
    own.start()
    for side in sides:
        @pl.when(jnp.logical_not(side[1]))
        def _():
            far_ref[side[4]] = jnp.zeros(far_ref.shape[1:], jnp.bfloat16)
    own.wait()
    for copy in copies:
        copy.wait()
    for side, edge in zip(sides, edges):
        pl.when(side[0])(edge.wait_send)
        pl.when(side[1])(edge.wait_recv)


def exchange(outgoing, ends, n_ctx):
    vmem = pl.BlockSpec(memory_space=pltpu.VMEM)
    return pl.pallas_call(
        functools.partial(exchange_kernel, n_ctx),
        in_specs=[vmem, vmem],
        out_specs=vmem,
        out_shape=jax.ShapeDtypeStruct((n_ctx + 2,) + outgoing.shape[1:], outgoing.dtype),
        scratch_shapes=[
            pltpu.SemaphoreType.DMA((n_ctx + 2,)),
            pltpu.SemaphoreType.DMA((n_ctx + 2,)),
            pltpu.SemaphoreType.DMA,
        ],
        compiler_params=pltpu.CompilerParams(
            collective_id=1, has_side_effects=True, vmem_limit_bytes=8 * 2**20
        ),
    )(outgoing, ends)


ROWS = 256


def encode_kernel(
    pick_ref, ids_ref, table_ref, weight_ref, bias_ref, gain_ref, shift_ref, qkv_ref,
    hidden_ref, query_ref, kv_ref, outgoing_ref, ends_ref, normed_ref,
):
    rows = ids_ref.shape[0]
    count = table_ref.shape[0]
    step = pl.program_id(0)
    own = table_ref[pl.ds(pl.multiple_of(EDGE + step * rows, EDGE), rows), :]
    conv = jnp.dot(own, weight_ref[0], preferred_element_type=jnp.float32)
    lane = lax.broadcasted_iota(jnp.int32, (rows, 128), 1)
    ids = ids_ref[...]
    for offset in range(6):
        column = jnp.broadcast_to(ids[:, offset : offset + 1], (rows, 128))
        low = column & 127
        high = (column >> 7).astype(jnp.float32).astype(jnp.bfloat16)
        hot = jnp.where(low == lane, 1.0, 0.0).astype(jnp.bfloat16)
        zero = jnp.zeros_like(hot)
        chosen = jnp.concatenate(
            [jnp.where(high == jnp.bfloat16(part), hot, zero) for part in range(count // 128)], 1
        )
        picked = jnp.dot(chosen, table_ref[...], preferred_element_type=jnp.float32)
        conv = conv + jnp.dot(
            picked.astype(jnp.bfloat16), weight_ref[offset + 1], preferred_element_type=jnp.float32
        )
    hidden = own.astype(jnp.float32) + conv + bias_ref[...]
    hidden_ref[...] = hidden
    center = hidden - jnp.mean(hidden, axis=-1, keepdims=True)
    variance = jnp.mean(center * center, axis=-1, keepdims=True)
    normed = (center * lax.rsqrt(variance + 1e-05) * gain_ref[...] + shift_ref[...]).astype(jnp.bfloat16)
    projected = jnp.dot(normed, qkv_ref[...], preferred_element_type=jnp.float32).astype(jnp.bfloat16)
    query_ref[...] = projected[:, :D]
    kv_ref[...] = projected[:, D:]
    normed_ref[pl.ds(pl.multiple_of(step * rows, rows), rows), :] = normed

    @pl.when(step == pl.num_programs(0) - 1)
    def _():
        ends_ref[0] = normed_ref[:BLK, :]
        ends_ref[1] = normed_ref[normed_ref.shape[0] - BLK :, :]
        for peer in range(outgoing_ref.shape[0]):
            first = pl.multiple_of(pick_ref[lax.axis_index("ctx"), peer] * BLK, BLK)
            outgoing_ref[peer] = normed_ref[pl.ds(first, BLK), :]


def encode(pick, ids, table, weight, bias, gain, shift, w_qkv):
    count, width = ids.shape[0], table.shape[1]
    whole = lambda shape: pl.BlockSpec(shape, lambda i, *_: (0,) * len(shape))
    tile = lambda cols: pl.BlockSpec((ROWS, cols), lambda i, *_: (i, 0))
    peers = pick.shape[0]
    return pl.pallas_call(
        encode_kernel,
        grid_spec=pltpu.PrefetchScalarGridSpec(
            num_scalar_prefetch=1,
            grid=(count // ROWS,),
            in_specs=[
                tile(6), whole(table.shape), whole(weight.shape),
                whole((1, width)), whole((1, width)), whole((1, width)), whole(w_qkv.shape),
            ],
            out_specs=[
                tile(width), tile(width), tile(2 * width),
                whole((peers, BLK, width)), whole((2, BLK, width)),
            ],
            scratch_shapes=[pltpu.VMEM((count, width), jnp.bfloat16)],
        ),
        out_shape=[
            jax.ShapeDtypeStruct((count, width), jnp.float32),
            jax.ShapeDtypeStruct((count, width), jnp.bfloat16),
            jax.ShapeDtypeStruct((count, 2 * width), jnp.bfloat16),
            jax.ShapeDtypeStruct((peers, BLK, width), jnp.bfloat16),
            jax.ShapeDtypeStruct((2, BLK, width), jnp.bfloat16),
        ],
        compiler_params=pltpu.CompilerParams(vmem_limit_bytes=20 * 2**20),
    )(pick, ids, table, weight, bias[None], gain[None], shift[None], w_qkv)


HALF = 128


def attend_kernel(
    slots_ref, lens_ref, pick_ref, query_ref, near_ref, far_ref, qkv_ref, hidden_ref, out_w_ref,
    out_ref, far_kv_ref, window_ref, keys_ref, values_ref,
):
    blk = pl.program_id(0)
    peers = pick_ref.shape[0]
    count = near_ref.shape[0]
    blocks = count // BLK
    ctx = lax.axis_index("ctx")

    @pl.when(blk == 0)
    def _():
        kv_weight = qkv_ref[:, D:]
        for peer in range(peers):
            far_kv_ref[peer * BLK : (peer + 1) * BLK, :] = jnp.dot(
                far_ref[peer], kv_weight, preferred_element_type=jnp.float32
            ).astype(jnp.bfloat16)
        window_ref[BLK : BLK + count, :] = near_ref[...]
        for side, first in ((peers, 0), (peers + 1, BLK + count)):
            window_ref[first : first + BLK, :] = jnp.dot(
                far_ref[side], kv_weight, preferred_element_type=jnp.float32
            ).astype(jnp.bfloat16)

        values_ref[:, :, HALF:] = jnp.ones((D // HALF, 7 * BLK, HALF), jnp.bfloat16)

    row = lax.broadcasted_iota(jnp.int32, (BLK, HALF), 0)
    lane = lax.broadcasted_iota(jnp.int32, (BLK, HALF), 1)
    for part in range(7):
        if part < 3:
            block = ctx * blocks + blk + part - 1
            inside = jnp.logical_and(block >= 0, block < peers * blocks)
            valid = jnp.where(inside, lens_ref[jnp.clip(block, 0, peers * blocks - 1)], 0)
            source = window_ref.at[pl.ds(pl.multiple_of((blk + part) * BLK, BLK), BLK)]
        else:
            slot = slots_ref[blk, part - 3]
            valid = lens_ref[slot * blocks + pick_ref[slot, ctx]]
            source = far_kv_ref.at[pl.ds(pl.multiple_of(slot * BLK, BLK), BLK)]
        masked = jnp.where(jnp.logical_and(row >= valid, lane == 0), -1e30, 0.0).astype(jnp.bfloat16)
        first = part * BLK
        for group in range(D // HALF):
            keys_ref[group, first : first + BLK, :HALF] = source[:, group * HALF : (group + 1) * HALF]
            keys_ref[group, first : first + BLK, HALF:] = masked
            values_ref[group, first : first + BLK, :HALF] = source[
                :, D + group * HALF : D + (group + 1) * HALF
            ]
    head_dim = D // HEADS
    head_of = lane // head_dim
    heads = HALF // head_dim
    adds_mask = jnp.where(lane == 0, 1.0, 0.0).astype(jnp.bfloat16)
    scale = math.log2(math.e) / math.sqrt(head_dim)
    halves = []
    for group in range(D // HALF):
        query = query_ref[:, group * HALF : (group + 1) * HALF]
        stacked = jnp.concatenate(
            [
                jnp.concatenate([jnp.where(head_of == head, query, jnp.zeros_like(query)), adds_mask], 1)
                for head in range(heads)
            ],
            0,
        )
        scores = lax.dot_general(
            stacked, keys_ref[group], (((1,), (1,)), ((), ())), preferred_element_type=jnp.float32
        )
        peak = jnp.max(scores, axis=-1, keepdims=True)
        weights = jnp.exp2((scores - peak) * scale).astype(jnp.bfloat16)
        mixed = jnp.dot(weights, values_ref[group], preferred_element_type=jnp.float32)
        mixed = mixed[:, :HALF] / mixed[:, HALF:]
        half = mixed[:BLK]
        for head in range(1, heads):
            half = jnp.where(head_of == head, mixed[head * BLK : (head + 1) * BLK], half)
        halves.append(half)
    attended = jnp.concatenate(halves, 1)
    out = hidden_ref[...] + jnp.dot(
        attended.astype(jnp.bfloat16), out_w_ref[...], preferred_element_type=jnp.float32
    )
    out_ref[...] = out.astype(jnp.bfloat16)


def attend(slots, lens, pick, queries, near, far, w_qkv, hidden, w_out):
    count, width = queries.shape
    whole = lambda shape: pl.BlockSpec(shape, lambda i, *_: (0,) * len(shape))
    tile = pl.BlockSpec((BLK, width), lambda i, *_: (i, 0))
    return pl.pallas_call(
        attend_kernel,
        grid_spec=pltpu.PrefetchScalarGridSpec(
            num_scalar_prefetch=3,
            grid=(count // BLK,),
            in_specs=[
                tile, whole(near.shape), whole(far.shape), whole(w_qkv.shape), tile, whole(w_out.shape)
            ],
            out_specs=tile,
            scratch_shapes=[
                pltpu.VMEM((pick.shape[0] * BLK, 2 * width), jnp.bfloat16),
                pltpu.VMEM((count + 2 * BLK, 2 * width), jnp.bfloat16),
                pltpu.VMEM((width // HALF, 7 * BLK, 2 * HALF), jnp.bfloat16),
                pltpu.VMEM((width // HALF, 7 * BLK, 2 * HALF), jnp.bfloat16),
            ],
        ),
        out_shape=jax.ShapeDtypeStruct((count, width), jnp.bfloat16),
        compiler_params=pltpu.CompilerParams(vmem_limit_bytes=32 * 2**20),
    )(slots, lens, pick, queries, near, far, w_qkv, hidden, w_out)


def on_device(
    feats,
    face_rows,
    neighbours,
    block_len,
    dilated,
    pick,
    cpe_weight,
    cpe_bias,
    ln_gain,
    ln_bias,
    w_qkv,
    w_out,
):
    voxels = feats[0]
    n_space, n_ctx = lax.axis_size("space"), lax.axis_size("ctx")
    table = build_table(face_rows[0], voxels, n_space, n_ctx)
    hidden, queries, near, outgoing, ends = encode(
        pick[0], neighbours[0], table, cpe_weight, cpe_bias, ln_gain, ln_bias, w_qkv
    )
    far = exchange(outgoing, ends, n_ctx)
    return attend(dilated[0], block_len[0], pick[0], queries, near, far, w_qkv, hidden, w_out)[None]


def solution(mesh):
    placed = (
        P("space", "ctx", None),
        P("space", "ctx"),
        P("space", "ctx", None),
        P("space", None),
        P("space", "ctx", None),
        P("space", None, None),
        P(),
        P(),
        P(),
        P(),
        P(),
        P(),
    )
    return jax.shard_map(
        on_device, mesh=mesh, in_specs=placed, out_specs=P("space", "ctx", None), check_vma=False
    )
```

```python
import functools
import math

import jax
import jax.numpy as jnp
from jax import lax
from jax.experimental import pallas as pl
from jax.experimental.pallas import tpu as pltpu
from jax.sharding import PartitionSpec as P

D = 256
HEADS = 8
BLK = 128
EDGE = 128
FACE = 256


MESH = pl.DeviceIdType.MESH


def table_kernel(n_space, n_ctx, rows_ref, own_ref, table_ref, face_ref, send_sem, recv_sem):
    space, ctx = lax.axis_index("space"), lax.axis_index("ctx")
    count = own_ref.shape[0]
    base = count + 2 * EDGE
    sides = (
        (ctx < n_ctx - 1, ctx > 0, (space, ctx + 1)),
        (ctx > 0, ctx < n_ctx - 1, (space, ctx - 1)),
        (space < n_space - 1, space > 0, (space + 1, ctx)),
        (space > 0, space < n_space - 1, (space - 1, ctx)),
    )
    barrier = pltpu.get_barrier_semaphore()
    for there, _, peer in sides:
        @pl.when(there)
        def _():
            pl.semaphore_signal(barrier, inc=1, device_id=peer, device_id_type=MESH)
    pl.semaphore_wait(barrier, sum(there.astype(jnp.int32) for there, _, _ in sides))
    targets = (
        (0, EDGE), (EDGE + count, EDGE), (base, FACE), (base + 2 * FACE, FACE)
    )
    sources = (
        own_ref.at[pl.ds(count - EDGE, EDGE)], own_ref.at[pl.ds(0, EDGE)], face_ref, face_ref
    )
    copies = [
        pltpu.make_async_remote_copy(
            src_ref=sources[i],
            dst_ref=table_ref.at[pl.ds(*targets[i])],
            send_sem=send_sem.at[i],
            recv_sem=recv_sem.at[i],
            device_id=sides[i][2],
            device_id_type=MESH,
        )
        for i in range(4)
    ]
    for i in (0, 1):
        pl.when(sides[i][0])(copies[i].start)
    place = lax.broadcasted_iota(jnp.int32, (FACE, count), 1)
    hot = jnp.where(rows_ref[...] == place, 1.0, 0.0).astype(jnp.bfloat16)
    face = jnp.dot(hot, own_ref[...], preferred_element_type=jnp.float32).astype(jnp.bfloat16)
    face_ref[...] = face
    for i in (2, 3):
        pl.when(sides[i][0])(copies[i].start)
    table_ref[EDGE : EDGE + count, :] = own_ref[...]
    table_ref[base + FACE : base + 2 * FACE, :] = face
    for i in range(4):
        first, width = targets[i]

        @pl.when(jnp.logical_not(sides[i][1]))
        def _():
            table_ref[first : first + width, :] = jnp.zeros((width, D), jnp.bfloat16)
    for i in range(4):
        pl.when(sides[i][0])(copies[i].wait_send)
        pl.when(sides[i][1])(copies[i].wait_recv)


def build_table(rows, own, n_space, n_ctx):
    count, width = own.shape
    vmem = pl.BlockSpec(memory_space=pltpu.VMEM)
    return pl.pallas_call(
        functools.partial(table_kernel, n_space, n_ctx),
        in_specs=[vmem, vmem],
        out_specs=vmem,
        out_shape=jax.ShapeDtypeStruct((count + 2 * EDGE + 3 * FACE, width), own.dtype),
        scratch_shapes=[
            pltpu.VMEM((FACE, width), own.dtype),
            pltpu.SemaphoreType.DMA((4,)),
            pltpu.SemaphoreType.DMA((4,)),
        ],
        compiler_params=pltpu.CompilerParams(
            collective_id=0, has_side_effects=True, vmem_limit_bytes=8 * 2**20
        ),
    )(rows[:, None], own)


def exchange_kernel(n_ctx, out_ref, ends_ref, far_ref, send_sem, recv_sem, local_sem):
    space, ctx = lax.axis_index("space"), lax.axis_index("ctx")
    barrier = pltpu.get_barrier_semaphore()
    for step in range(1, n_ctx):
        peer = lax.rem(ctx + step, n_ctx)
        pl.semaphore_signal(barrier, inc=1, device_id=(space, peer), device_id_type=MESH)
    pl.semaphore_wait(barrier, n_ctx - 1)
    copies = []
    for step in range(1, n_ctx):
        peer = lax.rem(ctx + step, n_ctx)
        copies.append(
            pltpu.make_async_remote_copy(
                src_ref=out_ref.at[peer],
                dst_ref=far_ref.at[ctx],
                send_sem=send_sem.at[step],
                recv_sem=recv_sem.at[step],
                device_id=(space, peer),
                device_id_type=MESH,
            )
        )
    sides = (
        (ctx < n_ctx - 1, ctx > 0, ctx + 1, 1, n_ctx),
        (ctx > 0, ctx < n_ctx - 1, ctx - 1, 0, n_ctx + 1),
    )
    edges = [
        pltpu.make_async_remote_copy(
            src_ref=ends_ref.at[source],
            dst_ref=far_ref.at[slot],
            send_sem=send_sem.at[slot],
            recv_sem=recv_sem.at[slot],
            device_id=(space, peer),
            device_id_type=MESH,
        )
        for _, _, peer, source, slot in sides
    ]
    order = sorted(range(1, n_ctx), key=lambda step: abs(step - n_ctx // 2))
    for step in order:
        copies[step - 1].start()
    for side, edge in zip(sides, edges):
        pl.when(side[0])(edge.start)
    own = pltpu.make_async_copy(out_ref.at[ctx], far_ref.at[ctx], local_sem)
    own.start()
    for side in sides:
        @pl.when(jnp.logical_not(side[1]))
        def _():
            far_ref[side[4]] = jnp.zeros(far_ref.shape[1:], jnp.bfloat16)
    own.wait()
    for copy in copies:
        copy.wait()
    for side, edge in zip(sides, edges):
        pl.when(side[0])(edge.wait_send)
        pl.when(side[1])(edge.wait_recv)


def exchange(outgoing, ends, n_ctx):
    vmem = pl.BlockSpec(memory_space=pltpu.VMEM)
    return pl.pallas_call(
        functools.partial(exchange_kernel, n_ctx),
        in_specs=[vmem, vmem],
        out_specs=vmem,
        out_shape=jax.ShapeDtypeStruct((n_ctx + 2,) + outgoing.shape[1:], outgoing.dtype),
        scratch_shapes=[
            pltpu.SemaphoreType.DMA((n_ctx + 2,)),
            pltpu.SemaphoreType.DMA((n_ctx + 2,)),
            pltpu.SemaphoreType.DMA,
        ],
        compiler_params=pltpu.CompilerParams(
            collective_id=1, has_side_effects=True, vmem_limit_bytes=8 * 2**20
        ),
    )(outgoing, ends)


ROWS = 1024


def encode_kernel(
    pick_ref, ids_ref, table_ref, weight_ref, bias_ref, gain_ref, shift_ref, qkv_ref,
    hidden_ref, query_ref, kv_ref, outgoing_ref, ends_ref, normed_ref,
):
    rows = ids_ref.shape[0]
    count = table_ref.shape[0]
    step = pl.program_id(0)
    own = table_ref[pl.ds(pl.multiple_of(EDGE + step * rows, EDGE), rows), :]
    conv = jnp.dot(own, weight_ref[0], preferred_element_type=jnp.float32)
    lane = lax.broadcasted_iota(jnp.int32, (rows, 128), 1)
    ids = ids_ref[...]
    for offset in range(6):
        column = jnp.broadcast_to(ids[:, offset : offset + 1], (rows, 128))
        low = column & 127
        high = (column >> 7).astype(jnp.float32).astype(jnp.bfloat16)
        hot = jnp.where(low == lane, 1.0, 0.0).astype(jnp.bfloat16)
        zero = jnp.zeros_like(hot)
        chosen = jnp.concatenate(
            [jnp.where(high == jnp.bfloat16(part), hot, zero) for part in range(count // 128)], 1
        )
        picked = jnp.dot(chosen, table_ref[...], preferred_element_type=jnp.float32)
        conv = conv + jnp.dot(
            picked.astype(jnp.bfloat16), weight_ref[offset + 1], preferred_element_type=jnp.float32
        )
    hidden = own.astype(jnp.float32) + conv + bias_ref[...]
    hidden_ref[...] = hidden
    center = hidden - jnp.mean(hidden, axis=-1, keepdims=True)
    variance = jnp.mean(center * center, axis=-1, keepdims=True)
    normed = (center * lax.rsqrt(variance + 1e-05) * gain_ref[...] + shift_ref[...]).astype(jnp.bfloat16)
    projected = jnp.dot(normed, qkv_ref[...], preferred_element_type=jnp.float32).astype(jnp.bfloat16)
    query_ref[...] = projected[:, :D]
    kv_ref[...] = projected[:, D:]
    normed_ref[pl.ds(pl.multiple_of(step * rows, rows), rows), :] = normed

    @pl.when(step == pl.num_programs(0) - 1)
    def _():
        ends_ref[0] = normed_ref[:BLK, :]
        ends_ref[1] = normed_ref[normed_ref.shape[0] - BLK :, :]
        for peer in range(outgoing_ref.shape[0]):
            first = pl.multiple_of(pick_ref[lax.axis_index("ctx"), peer] * BLK, BLK)
            outgoing_ref[peer] = normed_ref[pl.ds(first, BLK), :]


def encode(pick, ids, table, weight, bias, gain, shift, w_qkv):
    count, width = ids.shape[0], table.shape[1]
    whole = lambda shape: pl.BlockSpec(shape, lambda i, *_: (0,) * len(shape))
    tile = lambda cols: pl.BlockSpec((ROWS, cols), lambda i, *_: (i, 0))
    peers = pick.shape[0]
    return pl.pallas_call(
        encode_kernel,
        grid_spec=pltpu.PrefetchScalarGridSpec(
            num_scalar_prefetch=1,
            grid=(count // ROWS,),
            in_specs=[
                tile(6), whole(table.shape), whole(weight.shape),
                whole((1, width)), whole((1, width)), whole((1, width)), whole(w_qkv.shape),
            ],
            out_specs=[
                tile(width), tile(width), tile(2 * width),
                whole((peers, BLK, width)), whole((2, BLK, width)),
            ],
            scratch_shapes=[pltpu.VMEM((count, width), jnp.bfloat16)],
        ),
        out_shape=[
            jax.ShapeDtypeStruct((count, width), jnp.float32),
            jax.ShapeDtypeStruct((count, width), jnp.bfloat16),
            jax.ShapeDtypeStruct((count, 2 * width), jnp.bfloat16),
            jax.ShapeDtypeStruct((peers, BLK, width), jnp.bfloat16),
            jax.ShapeDtypeStruct((2, BLK, width), jnp.bfloat16),
        ],
        compiler_params=pltpu.CompilerParams(vmem_limit_bytes=20 * 2**20),
    )(pick, ids, table, weight, bias[None], gain[None], shift[None], w_qkv)


HALF = 128
CHUNK = 4
AHEAD = 1


def attend_kernel(
    slots_ref, lens_ref, pick_ref, query_ref, near_ref, far_ref, qkv_ref, hidden_ref, out_w_ref,
    out_ref, far_kv_ref, window_ref, keys_ref, values_ref,
):
    blk = pl.program_id(0)
    peers = pick_ref.shape[0]
    count = near_ref.shape[0]
    blocks = count // BLK
    ctx = lax.axis_index("ctx")

    @pl.when(blk == 0)
    def _():
        kv_weight = qkv_ref[:, D:]
        for peer in range(peers):
            far_kv_ref[peer * BLK : (peer + 1) * BLK, :] = jnp.dot(
                far_ref[peer], kv_weight, preferred_element_type=jnp.float32
            ).astype(jnp.bfloat16)
        window_ref[BLK : BLK + count, :] = near_ref[...]
        for side, first in ((peers, 0), (peers + 1, BLK + count)):
            window_ref[first : first + BLK, :] = jnp.dot(
                far_ref[side], kv_weight, preferred_element_type=jnp.float32
            ).astype(jnp.bfloat16)

        values_ref[:, :, HALF:] = jnp.ones((D // HALF, 7 * BLK, HALF), jnp.bfloat16)

    row = lax.broadcasted_iota(jnp.int32, (BLK, HALF), 0)
    lane = lax.broadcasted_iota(jnp.int32, (BLK, HALF), 1)
    for part in range(7):
        if part < 3:
            block = ctx * blocks + blk + part - 1
            inside = jnp.logical_and(block >= 0, block < peers * blocks)
            valid = jnp.where(inside, lens_ref[jnp.clip(block, 0, peers * blocks - 1)], 0)
            source = window_ref.at[pl.ds(pl.multiple_of((blk + part) * BLK, BLK), BLK)]
        else:
            slot = slots_ref[blk, part - 3]
            valid = lens_ref[slot * blocks + pick_ref[slot, ctx]]
            source = far_kv_ref.at[pl.ds(pl.multiple_of(slot * BLK, BLK), BLK)]
        masked = jnp.where(jnp.logical_and(row >= valid, lane == 0), -1e30, 0.0).astype(jnp.bfloat16)
        first = part * BLK
        for group in range(D // HALF):
            keys_ref[group, first : first + BLK, :HALF] = source[:, group * HALF : (group + 1) * HALF]
            keys_ref[group, first : first + BLK, HALF:] = masked
            values_ref[group, first : first + BLK, :HALF] = source[
                :, D + group * HALF : D + (group + 1) * HALF
            ]
    head_dim = D // HEADS
    head_of = lane // head_dim
    heads = HALF // head_dim
    adds_mask = jnp.where(lane == 0, 1.0, 0.0).astype(jnp.bfloat16)
    scale = math.log2(math.e) / math.sqrt(head_dim)
    chunks = [(group, first) for group in range(D // HALF) for first in range(0, heads, CHUNK)]

    def score(group, first):
        query = query_ref[:, group * HALF : (group + 1) * HALF]
        stacked = jnp.concatenate(
            [
                jnp.concatenate([jnp.where(head_of == head, query, jnp.zeros_like(query)), adds_mask], 1)
                for head in range(first, first + CHUNK)
            ],
            0,
        )
        return lax.dot_general(
            stacked, keys_ref[group], (((1,), (1,)), ((), ())), preferred_element_type=jnp.float32
        )

    halves = [jnp.zeros((BLK, HALF), jnp.float32) for _ in range(D // HALF)]
    ahead = [score(*chunk) for chunk in chunks[:AHEAD]]
    for turn, (group, first) in enumerate(chunks):
        if turn + AHEAD < len(chunks):
            ahead.append(score(*chunks[turn + AHEAD]))
        scores = ahead[turn]
        peak = jnp.max(scores, axis=-1, keepdims=True)
        weights = jnp.exp2((scores - peak) * scale).astype(jnp.bfloat16)
        mixed = jnp.dot(weights, values_ref[group], preferred_element_type=jnp.float32)
        mixed = mixed[:, :HALF] / mixed[:, HALF:]
        for head in range(CHUNK):
            halves[group] = jnp.where(
                head_of == first + head, mixed[head * BLK : (head + 1) * BLK], halves[group]
            )
    attended = jnp.concatenate(halves, 1)
    out = hidden_ref[...] + jnp.dot(
        attended.astype(jnp.bfloat16), out_w_ref[...], preferred_element_type=jnp.float32
    )
    out_ref[...] = out.astype(jnp.bfloat16)


def attend(slots, lens, pick, queries, near, far, w_qkv, hidden, w_out):
    count, width = queries.shape
    whole = lambda shape: pl.BlockSpec(shape, lambda i, *_: (0,) * len(shape))
    tile = pl.BlockSpec((BLK, width), lambda i, *_: (i, 0))
    return pl.pallas_call(
        attend_kernel,
        grid_spec=pltpu.PrefetchScalarGridSpec(
            num_scalar_prefetch=3,
            grid=(count // BLK,),
            in_specs=[
                tile, whole(near.shape), whole(far.shape), whole(w_qkv.shape), tile, whole(w_out.shape)
            ],
            out_specs=tile,
            scratch_shapes=[
                pltpu.VMEM((pick.shape[0] * BLK, 2 * width), jnp.bfloat16),
                pltpu.VMEM((count + 2 * BLK, 2 * width), jnp.bfloat16),
                pltpu.VMEM((width // HALF, 7 * BLK, 2 * HALF), jnp.bfloat16),
                pltpu.VMEM((width // HALF, 7 * BLK, 2 * HALF), jnp.bfloat16),
            ],
        ),
        out_shape=jax.ShapeDtypeStruct((count, width), jnp.bfloat16),
        compiler_params=pltpu.CompilerParams(vmem_limit_bytes=32 * 2**20),
    )(slots, lens, pick, queries, near, far, w_qkv, hidden, w_out)


def on_device(
    feats,
    face_rows,
    neighbours,
    block_len,
    dilated,
    pick,
    cpe_weight,
    cpe_bias,
    ln_gain,
    ln_bias,
    w_qkv,
    w_out,
):
    voxels = feats[0]
    n_space, n_ctx = lax.axis_size("space"), lax.axis_size("ctx")
    table = build_table(face_rows[0], voxels, n_space, n_ctx)
    hidden, queries, near, outgoing, ends = encode(
        pick[0], neighbours[0], table, cpe_weight, cpe_bias, ln_gain, ln_bias, w_qkv
    )
    far = exchange(outgoing, ends, n_ctx)
    return attend(dilated[0], block_len[0], pick[0], queries, near, far, w_qkv, hidden, w_out)[None]


def solution(mesh):
    placed = (
        P("space", "ctx", None),
        P("space", "ctx"),
        P("space", "ctx", None),
        P("space", None),
        P("space", "ctx", None),
        P("space", None, None),
        P(),
        P(),
        P(),
        P(),
        P(),
        P(),
    )
    return jax.shard_map(
        on_device, mesh=mesh, in_specs=placed, out_specs=P("space", "ctx", None), check_vma=False
    )
```

```python
import functools
import math

import jax
import jax.numpy as jnp
from jax import lax
from jax.experimental import pallas as pl
from jax.experimental.pallas import tpu as pltpu
from jax.sharding import PartitionSpec as P

D = 256
HEADS = 8
BLK = 128
EDGE = 128
FACE = 256


MESH = pl.DeviceIdType.MESH


def table_kernel(n_space, n_ctx, rows_ref, own_ref, table_ref, face_ref, send_sem, recv_sem):
    space, ctx = lax.axis_index("space"), lax.axis_index("ctx")
    count = own_ref.shape[0]
    base = count + 2 * EDGE
    sides = (
        (ctx < n_ctx - 1, ctx > 0, (space, ctx + 1)),
        (ctx > 0, ctx < n_ctx - 1, (space, ctx - 1)),
        (space < n_space - 1, space > 0, (space + 1, ctx)),
        (space > 0, space < n_space - 1, (space - 1, ctx)),
    )
    barrier = pltpu.get_barrier_semaphore()
    for there, _, peer in sides:
        @pl.when(there)
        def _():
            pl.semaphore_signal(barrier, inc=1, device_id=peer, device_id_type=MESH)
    pl.semaphore_wait(barrier, sum(there.astype(jnp.int32) for there, _, _ in sides))
    targets = (
        (0, EDGE), (EDGE + count, EDGE), (base, FACE), (base + 2 * FACE, FACE)
    )
    sources = (
        own_ref.at[pl.ds(count - EDGE, EDGE)], own_ref.at[pl.ds(0, EDGE)], face_ref, face_ref
    )
    copies = [
        pltpu.make_async_remote_copy(
            src_ref=sources[i],
            dst_ref=table_ref.at[pl.ds(*targets[i])],
            send_sem=send_sem.at[i],
            recv_sem=recv_sem.at[i],
            device_id=sides[i][2],
            device_id_type=MESH,
        )
        for i in range(4)
    ]
    for i in (0, 1):
        pl.when(sides[i][0])(copies[i].start)
    place = lax.broadcasted_iota(jnp.int32, (FACE, count), 1)
    hot = jnp.where(rows_ref[...] == place, 1.0, 0.0).astype(jnp.bfloat16)
    face = jnp.dot(hot, own_ref[...], preferred_element_type=jnp.float32).astype(jnp.bfloat16)
    face_ref[...] = face
    for i in (2, 3):
        pl.when(sides[i][0])(copies[i].start)
    table_ref[EDGE : EDGE + count, :] = own_ref[...]
    table_ref[base + FACE : base + 2 * FACE, :] = face
    for i in range(4):
        first, width = targets[i]

        @pl.when(jnp.logical_not(sides[i][1]))
        def _():
            table_ref[first : first + width, :] = jnp.zeros((width, D), jnp.bfloat16)
    for i in range(4):
        pl.when(sides[i][0])(copies[i].wait_send)
        pl.when(sides[i][1])(copies[i].wait_recv)


def build_table(rows, own, n_space, n_ctx):
    count, width = own.shape
    vmem = pl.BlockSpec(memory_space=pltpu.VMEM)
    return pl.pallas_call(
        functools.partial(table_kernel, n_space, n_ctx),
        in_specs=[vmem, vmem],
        out_specs=vmem,
        out_shape=jax.ShapeDtypeStruct((count + 2 * EDGE + 3 * FACE, width), own.dtype),
        scratch_shapes=[
            pltpu.VMEM((FACE, width), own.dtype),
            pltpu.SemaphoreType.DMA((4,)),
            pltpu.SemaphoreType.DMA((4,)),
        ],
        compiler_params=pltpu.CompilerParams(
            collective_id=0, has_side_effects=True, vmem_limit_bytes=8 * 2**20
        ),
    )(rows[:, None], own)


def exchange_kernel(n_ctx, out_ref, ends_ref, far_ref, send_sem, recv_sem, local_sem):
    space, ctx = lax.axis_index("space"), lax.axis_index("ctx")
    barrier = pltpu.get_barrier_semaphore()
    for step in range(1, n_ctx):
        peer = lax.rem(ctx + step, n_ctx)
        pl.semaphore_signal(barrier, inc=1, device_id=(space, peer), device_id_type=MESH)
    pl.semaphore_wait(barrier, n_ctx - 1)
    copies = []
    for step in range(1, n_ctx):
        peer = lax.rem(ctx + step, n_ctx)
        copies.append(
            pltpu.make_async_remote_copy(
                src_ref=out_ref.at[peer],
                dst_ref=far_ref.at[ctx],
                send_sem=send_sem.at[step],
                recv_sem=recv_sem.at[step],
                device_id=(space, peer),
                device_id_type=MESH,
            )
        )
    sides = (
        (ctx < n_ctx - 1, ctx > 0, ctx + 1, 1, n_ctx),
        (ctx > 0, ctx < n_ctx - 1, ctx - 1, 0, n_ctx + 1),
    )
    edges = [
        pltpu.make_async_remote_copy(
            src_ref=ends_ref.at[source],
            dst_ref=far_ref.at[slot],
            send_sem=send_sem.at[slot],
            recv_sem=recv_sem.at[slot],
            device_id=(space, peer),
            device_id_type=MESH,
        )
        for _, _, peer, source, slot in sides
    ]
    order = sorted(range(1, n_ctx), key=lambda step: abs(step - n_ctx // 2))
    for step in order:
        copies[step - 1].start()
    for side, edge in zip(sides, edges):
        pl.when(side[0])(edge.start)
    own = pltpu.make_async_copy(out_ref.at[ctx], far_ref.at[ctx], local_sem)
    own.start()
    for side in sides:
        @pl.when(jnp.logical_not(side[1]))
        def _():
            far_ref[side[4]] = jnp.zeros(far_ref.shape[1:], jnp.bfloat16)
    own.wait()
    for copy in copies:
        copy.wait()
    for side, edge in zip(sides, edges):
        pl.when(side[0])(edge.wait_send)
        pl.when(side[1])(edge.wait_recv)


def exchange(outgoing, ends, n_ctx):
    vmem = pl.BlockSpec(memory_space=pltpu.VMEM)
    return pl.pallas_call(
        functools.partial(exchange_kernel, n_ctx),
        in_specs=[vmem, vmem],
        out_specs=vmem,
        out_shape=jax.ShapeDtypeStruct((n_ctx + 2,) + outgoing.shape[1:], outgoing.dtype),
        scratch_shapes=[
            pltpu.SemaphoreType.DMA((n_ctx + 2,)),
            pltpu.SemaphoreType.DMA((n_ctx + 2,)),
            pltpu.SemaphoreType.DMA,
        ],
        compiler_params=pltpu.CompilerParams(
            collective_id=1, has_side_effects=True, vmem_limit_bytes=8 * 2**20
        ),
    )(outgoing, ends)


ROWS = 1024


def encode_kernel(
    pick_ref, ids_ref, table_ref, weight_ref, bias_ref, gain_ref, shift_ref, qkv_ref,
    hidden_ref, query_ref, kv_ref, outgoing_ref, ends_ref, normed_ref,
):
    rows = ids_ref.shape[0]
    count = table_ref.shape[0]
    step = pl.program_id(0)
    own = table_ref[pl.ds(pl.multiple_of(EDGE + step * rows, EDGE), rows), :]
    conv = jnp.dot(own, weight_ref[0], preferred_element_type=jnp.float32)
    lane = lax.broadcasted_iota(jnp.int32, (rows, 128), 1)
    ids = ids_ref[...]
    for offset in range(6):
        column = jnp.broadcast_to(ids[:, offset : offset + 1], (rows, 128))
        low = column & 127
        high = (column >> 7).astype(jnp.float32).astype(jnp.bfloat16)
        hot = jnp.where(low == lane, 1.0, 0.0).astype(jnp.bfloat16)
        zero = jnp.zeros_like(hot)
        chosen = jnp.concatenate(
            [jnp.where(high == jnp.bfloat16(part), hot, zero) for part in range(count // 128)], 1
        )
        picked = jnp.dot(chosen, table_ref[...], preferred_element_type=jnp.float32)
        conv = conv + jnp.dot(
            picked.astype(jnp.bfloat16), weight_ref[offset + 1], preferred_element_type=jnp.float32
        )
    hidden = own.astype(jnp.float32) + conv + bias_ref[...]
    hidden_ref[...] = hidden
    center = hidden - jnp.mean(hidden, axis=-1, keepdims=True)
    variance = jnp.mean(center * center, axis=-1, keepdims=True)
    normed = (center * lax.rsqrt(variance + 1e-05) * gain_ref[...] + shift_ref[...]).astype(jnp.bfloat16)
    projected = jnp.dot(normed, qkv_ref[...], preferred_element_type=jnp.float32).astype(jnp.bfloat16)
    query_ref[...] = projected[:, :D]
    kv_ref[...] = projected[:, D:]
    normed_ref[pl.ds(pl.multiple_of(step * rows, rows), rows), :] = normed

    @pl.when(step == pl.num_programs(0) - 1)
    def _():
        ends_ref[0] = normed_ref[:BLK, :]
        ends_ref[1] = normed_ref[normed_ref.shape[0] - BLK :, :]
        for peer in range(outgoing_ref.shape[0]):
            first = pl.multiple_of(pick_ref[lax.axis_index("ctx"), peer] * BLK, BLK)
            outgoing_ref[peer] = normed_ref[pl.ds(first, BLK), :]


def encode(pick, ids, table, weight, bias, gain, shift, w_qkv):
    count, width = ids.shape[0], table.shape[1]
    whole = lambda shape: pl.BlockSpec(shape, lambda i, *_: (0,) * len(shape))
    tile = lambda cols: pl.BlockSpec((ROWS, cols), lambda i, *_: (i, 0))
    peers = pick.shape[0]
    return pl.pallas_call(
        encode_kernel,
        grid_spec=pltpu.PrefetchScalarGridSpec(
            num_scalar_prefetch=1,
            grid=(count // ROWS,),
            in_specs=[
                tile(6), whole(table.shape), whole(weight.shape),
                whole((1, width)), whole((1, width)), whole((1, width)), whole(w_qkv.shape),
            ],
            out_specs=[
                tile(width), tile(width), tile(2 * width),
                whole((peers, BLK, width)), whole((2, BLK, width)),
            ],
            scratch_shapes=[pltpu.VMEM((count, width), jnp.bfloat16)],
        ),
        out_shape=[
            pltpu.HBM((count, width), jnp.float32),
            jax.ShapeDtypeStruct((count, width), jnp.bfloat16),
            jax.ShapeDtypeStruct((count, 2 * width), jnp.bfloat16),
            jax.ShapeDtypeStruct((peers, BLK, width), jnp.bfloat16),
            jax.ShapeDtypeStruct((2, BLK, width), jnp.bfloat16),
        ],
        compiler_params=pltpu.CompilerParams(vmem_limit_bytes=20 * 2**20),
    )(pick, ids, table, weight, bias[None], gain[None], shift[None], w_qkv)


HALF = 128
CHUNK = 4
AHEAD = 1


def attend_kernel(
    slots_ref, lens_ref, pick_ref, query_ref, near_ref, far_ref, qkv_ref, hidden_ref, out_w_ref,
    out_ref, far_kv_ref, window_ref, keys_ref, values_ref,
):
    blk = pl.program_id(0)
    peers = pick_ref.shape[0]
    count = near_ref.shape[0]
    blocks = count // BLK
    ctx = lax.axis_index("ctx")

    @pl.when(blk == 0)
    def _():
        kv_weight = qkv_ref[:, D:]
        for peer in range(peers):
            far_kv_ref[peer * BLK : (peer + 1) * BLK, :] = jnp.dot(
                far_ref[peer], kv_weight, preferred_element_type=jnp.float32
            ).astype(jnp.bfloat16)
        window_ref[BLK : BLK + count, :] = near_ref[...]
        for side, first in ((peers, 0), (peers + 1, BLK + count)):
            window_ref[first : first + BLK, :] = jnp.dot(
                far_ref[side], kv_weight, preferred_element_type=jnp.float32
            ).astype(jnp.bfloat16)

        values_ref[:, :, HALF:] = jnp.ones((D // HALF, 7 * BLK, HALF), jnp.bfloat16)

    row = lax.broadcasted_iota(jnp.int32, (BLK, HALF), 0)
    lane = lax.broadcasted_iota(jnp.int32, (BLK, HALF), 1)
    for part in range(7):
        if part < 3:
            block = ctx * blocks + blk + part - 1
            inside = jnp.logical_and(block >= 0, block < peers * blocks)
            valid = jnp.where(inside, lens_ref[jnp.clip(block, 0, peers * blocks - 1)], 0)
            source = window_ref.at[pl.ds(pl.multiple_of((blk + part) * BLK, BLK), BLK)]
        else:
            slot = slots_ref[blk, part - 3]
            valid = lens_ref[slot * blocks + pick_ref[slot, ctx]]
            source = far_kv_ref.at[pl.ds(pl.multiple_of(slot * BLK, BLK), BLK)]
        masked = jnp.where(jnp.logical_and(row >= valid, lane == 0), -1e30, 0.0).astype(jnp.bfloat16)
        first = part * BLK
        for group in range(D // HALF):
            keys_ref[group, first : first + BLK, :HALF] = source[:, group * HALF : (group + 1) * HALF]
            keys_ref[group, first : first + BLK, HALF:] = masked
            values_ref[group, first : first + BLK, :HALF] = source[
                :, D + group * HALF : D + (group + 1) * HALF
            ]
    head_dim = D // HEADS
    head_of = lane // head_dim
    heads = HALF // head_dim
    adds_mask = jnp.where(lane == 0, 1.0, 0.0).astype(jnp.bfloat16)
    scale = math.log2(math.e) / math.sqrt(head_dim)
    chunks = [(group, first) for group in range(D // HALF) for first in range(0, heads, CHUNK)]

    def score(group, first):
        query = query_ref[:, group * HALF : (group + 1) * HALF]
        stacked = jnp.concatenate(
            [
                jnp.concatenate([jnp.where(head_of == head, query, jnp.zeros_like(query)), adds_mask], 1)
                for head in range(first, first + CHUNK)
            ],
            0,
        )
        return lax.dot_general(
            stacked, keys_ref[group], (((1,), (1,)), ((), ())), preferred_element_type=jnp.float32
        )

    halves = [jnp.zeros((BLK, HALF), jnp.float32) for _ in range(D // HALF)]
    ahead = [score(*chunk) for chunk in chunks[:AHEAD]]
    for turn, (group, first) in enumerate(chunks):
        if turn + AHEAD < len(chunks):
            ahead.append(score(*chunks[turn + AHEAD]))
        scores = ahead[turn]
        peak = jnp.max(scores, axis=-1, keepdims=True)
        weights = jnp.exp2((scores - peak) * scale).astype(jnp.bfloat16)
        mixed = jnp.dot(weights, values_ref[group], preferred_element_type=jnp.float32)
        mixed = mixed[:, :HALF] / mixed[:, HALF:]
        for head in range(CHUNK):
            halves[group] = jnp.where(
                head_of == first + head, mixed[head * BLK : (head + 1) * BLK], halves[group]
            )
    attended = jnp.concatenate(halves, 1)
    out = hidden_ref[...] + jnp.dot(
        attended.astype(jnp.bfloat16), out_w_ref[...], preferred_element_type=jnp.float32
    )
    out_ref[...] = out.astype(jnp.bfloat16)


def attend(slots, lens, pick, queries, near, far, w_qkv, hidden, w_out):
    count, width = queries.shape
    whole = lambda shape: pl.BlockSpec(shape, lambda i, *_: (0,) * len(shape))
    tile = pl.BlockSpec((BLK, width), lambda i, *_: (i, 0))
    return pl.pallas_call(
        attend_kernel,
        grid_spec=pltpu.PrefetchScalarGridSpec(
            num_scalar_prefetch=3,
            grid=(count // BLK,),
            in_specs=[
                tile, whole(near.shape), whole(far.shape), whole(w_qkv.shape), tile, whole(w_out.shape)
            ],
            out_specs=tile,
            scratch_shapes=[
                pltpu.VMEM((pick.shape[0] * BLK, 2 * width), jnp.bfloat16),
                pltpu.VMEM((count + 2 * BLK, 2 * width), jnp.bfloat16),
                pltpu.VMEM((width // HALF, 7 * BLK, 2 * HALF), jnp.bfloat16),
                pltpu.VMEM((width // HALF, 7 * BLK, 2 * HALF), jnp.bfloat16),
            ],
        ),
        out_shape=jax.ShapeDtypeStruct((count, width), jnp.bfloat16),
        compiler_params=pltpu.CompilerParams(vmem_limit_bytes=32 * 2**20),
    )(slots, lens, pick, queries, near, far, w_qkv, hidden, w_out)


def on_device(
    feats,
    face_rows,
    neighbours,
    block_len,
    dilated,
    pick,
    cpe_weight,
    cpe_bias,
    ln_gain,
    ln_bias,
    w_qkv,
    w_out,
):
    voxels = feats[0]
    n_space, n_ctx = lax.axis_size("space"), lax.axis_size("ctx")
    table = build_table(face_rows[0], voxels, n_space, n_ctx)
    hidden, queries, near, outgoing, ends = encode(
        pick[0], neighbours[0], table, cpe_weight, cpe_bias, ln_gain, ln_bias, w_qkv
    )
    hidden = pltpu.with_memory_space_constraint(hidden, pltpu.HBM)
    far = exchange(outgoing, ends, n_ctx)
    return attend(dilated[0], block_len[0], pick[0], queries, near, far, w_qkv, hidden, w_out)[None]


def solution(mesh):
    placed = (
        P("space", "ctx", None),
        P("space", "ctx"),
        P("space", "ctx", None),
        P("space", None),
        P("space", "ctx", None),
        P("space", None, None),
        P(),
        P(),
        P(),
        P(),
        P(),
        P(),
    )
    return jax.shard_map(
        on_device, mesh=mesh, in_specs=placed, out_specs=P("space", "ctx", None), check_vma=False
    )
```
